128 devices in a mesh: row: 4 (over y_hi, core), col: 32 (over z, y_lo, x).
Axes of the slice: x: 4, y: 4 (y_hi: 2, y_lo: 2; y = y_hi * 2 + y_lo), z: 4, core: 2. Of those that a mesh axis runs over, the one named last changes fastest.
Arguments:
- slopes: float32 [1024, 131072], P('col', 'row'), may hold values from -6 to 6
- covariance: float32 [2048, 131072], P('row', 'col'), may hold values from -6 to 6
Outputs:
- updated: float32 [2048, 131072], P('row', 'col')
The draws below stay inside these ranges and needn't reach their ends.
All inputs are finite; a program needn't handle non-finite values.
Results may differ from the reference program's by a relative error of at most 0.00007.
Values sent between devices are 32-bit elements; how exact they have to be, the bound alone decides.
A program may use at most 192 MiB of HBM per device.

```python
import jax
import jax.numpy as jnp
from jax import lax

SLOPES = 131072
ROWS = 2048
FRAMES = 1024


def shard_levels(rng, extent, split, least, high):
    factor_of = 1.0
    for axis_at, shards_of in split:
        draws = jax.random.uniform(jax.random.fold_in(jax.random.fold_in(rng, 6), axis_at), (shards_of,), jnp.float32, least / len(split), high / len(split))
        factor_of = factor_of * jnp.repeat(jnp.exp(draws), extent[axis_at] // shards_of).reshape((-1,) + (1,) * (len(extent) - 1 - axis_at))
    return factor_of


def noise(stream_key, shape, spread, most, shards=(), held_as=jnp.bfloat16):
    level = shard_levels(stream_key, shape, shards, -0.22, 0.18) if shards else 1.0
    values = jax.random.normal(stream_key, shape, jnp.float32) * spread * level
    return jnp.minimum(jnp.maximum(values, -most), most).astype(held_as)


def setup_inputs(seed: int = 0) -> dict:
    splits = jax.random.split(jax.random.key(seed), 3)
    return {
        "slopes": noise(splits[0], (FRAMES, SLOPES), 1.0, 6.0, ((0, 32), (1, 4)), jnp.float32),
        "covariance": noise(splits[1], (ROWS, SLOPES), 1.0, 6.0, ((0, 4), (1, 32)), jnp.float32),
    }


def reference(slopes, covariance):
    slab = slopes[:, :ROWS]
    product = lax.dot_general(slab, slopes, (((0,), (0,)), ((), ())), precision=lax.Precision.HIGHEST, preferred_element_type=jnp.float32)
    return covariance + product / jnp.sqrt(jnp.float32(FRAMES))
```

```python
import functools

import jax
import jax.numpy as jnp
from jax import lax
from jax.experimental import pallas as pl
from jax.experimental.pallas import tpu as pltpu
from jax.sharding import PartitionSpec as P

MESH = pl.DeviceIdType.MESH
WIDTH = 256
AHEAD = 3
LAG = 3


def kernel(
    slopes, cov, out, held, tall, slab, slab_hi, slab_lo,
    sx, rx, sy, ry, sf, rf, ss, rs, own_sem, cov_sem,
):
    row, col = lax.axis_index("row"), lax.axis_index("col")
    x, y_lo, z = lax.rem(col, 4), lax.rem(lax.div(col, 4), 2), lax.div(col, 8)
    core, y_hi = lax.rem(row, 2), lax.div(row, 2)
    tiles, frames, width = tall.shape
    half = frames // 2
    block = tiles * width
    depth = slab.shape[3]

    def at(dx, dz):
        return lax.rem(z + dz, 4) * 8 + y_lo * 4 + lax.rem(x + dx, 4)

    barrier = pltpu.get_barrier_semaphore()
    for dr in range(4):
        for dc in range(8):
            if dr or dc:
                there = lax.rem(dc + y_lo + 2 * z, 8)
                pl.semaphore_signal(
                    barrier, inc=1,
                    device_id=(lax.rem(row + dr, 4), there * 4 + x),
                    device_id_type=MESH,
                )
    for dx in range(1, 4):
        pl.semaphore_signal(barrier, inc=1, device_id=(row, at(dx, 0)), device_id_type=MESH)
    pl.semaphore_wait(barrier, 34)

    def remote(src, dst, send, recv, r, c):
        return pltpu.make_async_remote_copy(
            src_ref=src, dst_ref=dst, send_sem=send, recv_sem=recv,
            device_id=(r, c), device_id_type=MESH,
        )

    cov_copy = pltpu.make_async_copy(cov, out, cov_sem)

    is_source = row < 2
    is_source = jnp.logical_and(is_source, core == 0)

    def slab_columns(r):
        return slopes.at[:, pl.ds(pl.multiple_of(r * 512, 512), 512)]

    @pl.when(is_source)
    def _():
        mine = slab.at[y_lo, z, x]
        for dr in range(4):
            for dl in range(2):
                r, l = lax.rem(row + dr, 4), lax.rem(y_lo + dl, 2)
                if dr == 0 and dl == 0:
                    pltpu.make_async_copy(slab_columns(r), mine, rs.at[0]).start()
                else:
                    remote(slab_columns(r), mine, ss.at[0], rs.at[0], r, z * 8 + l * 4 + x).start()

    def slab_z():
        return [
            remote(slab.at[:, z, x], slab.at[:, z, x], ss.at[1], rs.at[1], row, at(0, dz))
            for dz in range(1, 4)
        ]

    def slab_x():
        return [
            remote(slab.at[:, :, x], slab.at[:, :, x], ss.at[2], rs.at[2], row, at(dx, 0))
            for dx in range(1, 4)
        ]

    def wait_for(ref, sem):
        pltpu.make_async_copy(ref, ref, sem).wait()

    def send_x(t):
        for l in range(2):
            for dx in range(4):
                to = lax.rem(x + dx, 4)
                first = pl.multiple_of((l * 4 + to) * block + t * width, width)
                src = slopes.at[:, pl.ds(first, width)]
                dst = held.at[t, l, pl.ds(pl.multiple_of(x * depth, depth), depth)]
                if dx == 0:
                    pltpu.make_async_copy(src, dst, rx.at[t]).start()
                else:
                    remote(src, dst, sx.at[t], rx.at[t], row, at(dx, 0)).start()

    def yz(t, dh, l, start):
        h = lax.rem(y_hi + dh, 2)
        src = held.at[t, l]
        dst = tall.at[t, pl.ds(pl.multiple_of(y_lo * half + z * 128, 128), 128)]
        r, c = h * 2 + y_lo, row * 8 + l * 4 + x
        is_self = jnp.logical_and(r == row, c == col)

        if start:

            @pl.when(is_self)
            def _():
                pltpu.make_async_copy(src, dst, ry.at[t]).start()

        @pl.when(jnp.logical_not(is_self))
        def _():
            copy = remote(src, dst, sy.at[t], ry.at[t], r, c)
            if start:
                copy.start()
            else:
                copy.wait_send()

    def send_yz(t):
        for dh in (1, 0):
            for l in range(2):
                yz(t, dh, l, True)

    def group(t, g):
        return tall.at[t, pl.ds(pl.multiple_of(g * half, half), half)]

    def forward(t):
        mine = group(t, core)
        return remote(mine, mine, sf.at[t], rf.at[t], y_hi * 2 + 1 - core, col)

    def compute(t):
        tile = tall[t]
        hi = tile.astype(jnp.bfloat16)
        lo = (tile - hi.astype(jnp.float32)).astype(jnp.bfloat16)
        dot = functools.partial(jnp.dot, preferred_element_type=jnp.float32)
        product = dot(slab_hi[...], hi) + dot(slab_hi[...], lo) + dot(slab_lo[...], hi)
        columns = pl.ds(pl.multiple_of(t * width, width), width)
        out[:, columns] = out[:, columns] + product * (1.0 / frames**0.5)

    for t in range(AHEAD):
        send_x(t)
    cov_copy.start()
    wait_for(slab.at[:, z, x], rs.at[0])
    for copy in slab_z():
        copy.start()

    def prepare():
        cov_copy.wait()
        wait_for(slab.at[:, :, pl.ds(0, 3)], rs.at[2])
        for l in range(2):
            whole = slab[l].reshape(half, 512).T
            hi = whole.astype(jnp.bfloat16)
            columns = pl.ds(l * half, half)
            slab_hi[:, columns] = hi
            slab_lo[:, columns] = (whole - hi.astype(jnp.float32)).astype(jnp.bfloat16)

    @pl.loop(0, tiles + LAG + 1)
    def _(s):
        @pl.when(s < tiles)
        def _():
            wait_for(held.at[s], rx.at[s])
            send_yz(s)

        @pl.when(s + AHEAD < tiles)
        def _():
            send_x(s + AHEAD)

        @pl.when(s == 0)
        def _():
            wait_for(slab.at[:, pl.ds(0, 3), x], rs.at[1])
            for copy in slab_x():
                copy.start()

        @pl.when(jnp.logical_and(s >= LAG, s < tiles + LAG))
        def _():
            u = s - LAG
            wait_for(group(u, core), ry.at[u])
            forward(u).start()

        @pl.when(s == LAG)
        def _():
            prepare()

        @pl.when(s > LAG)
        def _():
            v = s - LAG - 1
            wait_for(group(v, 1 - core), rf.at[v])
            compute(v)

    @pl.when(is_source)
    def _():
        wait_for(tall.at[0, pl.ds(0, 7 * 64)], ss.at[0])
    for copy in slab_z():
        copy.wait_send()
    for copy in slab_x():
        copy.wait_send()

    @pl.loop(0, tiles)
    def _(t):
        wait_for(held.at[t].at[:, 0:96], sx.at[t])
        for dh in (1, 0):
            for l in range(2):
                yz(t, dh, l, False)
        forward(t).wait_send()


def per_device(slopes, covariance):
    frames, columns, rows = 1024, covariance.shape[1], covariance.shape[0]
    tiles = columns // WIDTH
    vmem = pl.BlockSpec(memory_space=pltpu.VMEM)
    hbm = pl.BlockSpec(memory_space=pl.ANY)
    dma = pltpu.SemaphoreType.DMA
    return pl.pallas_call(
        kernel,
        out_shape=jax.ShapeDtypeStruct(covariance.shape, jnp.float32),
        in_specs=[hbm, hbm],
        out_specs=vmem,
        scratch_shapes=[
            pltpu.VMEM((tiles, 2, 128, WIDTH), jnp.float32),
            pltpu.VMEM((tiles, frames, WIDTH), jnp.float32),
            pltpu.VMEM((2, 4, 4, 32, rows), jnp.float32),
            pltpu.VMEM((rows, frames), jnp.bfloat16),
            pltpu.VMEM((rows, frames), jnp.bfloat16),
            dma((tiles,)), dma((tiles,)), dma((tiles,)), dma((tiles,)), dma((tiles,)), dma((tiles,)),
            dma((3,)), dma((3,)), dma, dma,
        ],
        compiler_params=pltpu.CompilerParams(
            collective_id=0, has_side_effects=True, vmem_limit_bytes=50 << 20
        ),
        cost_estimate=pl.CostEstimate(
            flops=6 * rows * frames * columns, bytes_accessed=24 << 20, transcendentals=0
        ),
        name="slab_update",
    )(slopes, covariance)


def solution(mesh):
    return jax.shard_map(
        per_device, mesh=mesh, in_specs=(P("col", "row"), P("row", "col")),
        out_specs=P("row", "col"), check_vma=False,
    )
```

```python
import functools

import jax
import jax.numpy as jnp
from jax import lax
from jax.experimental import pallas as pl
from jax.experimental.pallas import tpu as pltpu
from jax.sharding import PartitionSpec as P

MESH = pl.DeviceIdType.MESH
WIDTH = 256
AHEAD = 6
LAG = 6


def kernel(
    slopes, cov, out, held, tall, slab, slab_hi, slab_lo,
    sx, rx, sy, ry, sf, rf, ss, rs, own_sem, cov_sem,
):
    row, col = lax.axis_index("row"), lax.axis_index("col")
    x, y_lo, z = lax.rem(col, 4), lax.rem(lax.div(col, 4), 2), lax.div(col, 8)
    core, y_hi = lax.rem(row, 2), lax.div(row, 2)
    tiles, frames, width = tall.shape
    half = frames // 2
    block = tiles * width
    depth = slab.shape[3]

    def at(dx, dz):
        return lax.rem(z + dz, 4) * 8 + y_lo * 4 + lax.rem(x + dx, 4)

    barrier = pltpu.get_barrier_semaphore()
    for dr in range(4):
        for dc in range(8):
            if dr or dc:
                there = lax.rem(dc + y_lo + 2 * z, 8)
                pl.semaphore_signal(
                    barrier, inc=1,
                    device_id=(lax.rem(row + dr, 4), there * 4 + x),
                    device_id_type=MESH,
                )
    for dx in range(1, 4):
        pl.semaphore_signal(barrier, inc=1, device_id=(row, at(dx, 0)), device_id_type=MESH)
    pl.semaphore_wait(barrier, 34)

    def remote(src, dst, send, recv, r, c):
        return pltpu.make_async_remote_copy(
            src_ref=src, dst_ref=dst, send_sem=send, recv_sem=recv,
            device_id=(r, c), device_id_type=MESH,
        )

    cov_copy = pltpu.make_async_copy(cov, out, cov_sem)

    is_source = row < 2
    is_source = jnp.logical_and(is_source, core == 0)

    def slab_columns(r):
        return slopes.at[:, pl.ds(pl.multiple_of(r * 512, 512), 512)]

    @pl.when(is_source)
    def _():
        mine = slab.at[y_lo, z, x]
        for dr in range(4):
            for dl in range(2):
                r, l = lax.rem(row + dr, 4), lax.rem(y_lo + dl, 2)
                if dr == 0 and dl == 0:
                    pltpu.make_async_copy(slab_columns(r), mine, rs.at[0]).start()
                else:
                    remote(slab_columns(r), mine, ss.at[0], rs.at[0], r, z * 8 + l * 4 + x).start()

    def slab_z():
        return [
            remote(slab.at[:, z, x], slab.at[:, z, x], ss.at[1], rs.at[1], row, at(0, dz))
            for dz in range(1, 4)
        ]

    def slab_x():
        return [
            remote(slab.at[:, :, x], slab.at[:, :, x], ss.at[2], rs.at[2], row, at(dx, 0))
            for dx in range(1, 4)
        ]

    def wait_for(ref, sem):
        pltpu.make_async_copy(ref, ref, sem).wait()

    def send_x(t):
        for l in range(2):
            for dx in range(4):
                to = lax.rem(x + dx, 4)
                first = pl.multiple_of((l * 4 + to) * block + t * width, width)
                src = slopes.at[:, pl.ds(first, width)]
                dst = held.at[t, l, pl.ds(pl.multiple_of(x * depth, depth), depth)]
                if dx == 0:
                    pltpu.make_async_copy(src, dst, rx.at[t]).start()
                else:
                    remote(src, dst, sx.at[t], rx.at[t], row, at(dx, 0)).start()

    def yz(t, dh, l, start):
        h = lax.rem(y_hi + dh, 2)
        src = held.at[t, l]
        dst = tall.at[t, pl.ds(pl.multiple_of(y_lo * half + z * 128, 128), 128)]
        r, c = h * 2 + y_lo, row * 8 + l * 4 + x
        is_self = jnp.logical_and(r == row, c == col)

        if start:

            @pl.when(is_self)
            def _():
                pltpu.make_async_copy(src, dst, ry.at[t]).start()

        @pl.when(jnp.logical_not(is_self))
        def _():
            copy = remote(src, dst, sy.at[t], ry.at[t], r, c)
            if start:
                copy.start()
            else:
                copy.wait_send()

    def send_yz(t):
        for dh in (1, 0):
            for l in range(2):
                yz(t, dh, l, True)

    def group(t, g):
        return tall.at[t, pl.ds(pl.multiple_of(g * half, half), half)]

    def forward(t):
        mine = group(t, core)
        return remote(mine, mine, sf.at[t], rf.at[t], y_hi * 2 + 1 - core, col)

    def compute(t):
        tile = tall[t]
        hi = tile.astype(jnp.bfloat16)
        lo = (tile - hi.astype(jnp.float32)).astype(jnp.bfloat16)
        dot = functools.partial(jnp.dot, preferred_element_type=jnp.float32)
        product = dot(slab_hi[...], hi) + dot(slab_hi[...], lo) + dot(slab_lo[...], hi)
        columns = pl.ds(pl.multiple_of(t * width, width), width)
        out[:, columns] = out[:, columns] + product * (1.0 / frames**0.5)

    for t in range(AHEAD):
        send_x(t)
    cov_copy.start()
    wait_for(slab.at[:, z, x], rs.at[0])
    for copy in slab_z():
        copy.start()

    def prepare():
        cov_copy.wait()
        wait_for(slab.at[:, :, pl.ds(0, 3)], rs.at[2])
        for l in range(2):
            whole = slab[l].reshape(half, 512).T
            hi = whole.astype(jnp.bfloat16)
            columns = pl.ds(l * half, half)
            slab_hi[:, columns] = hi
            slab_lo[:, columns] = (whole - hi.astype(jnp.float32)).astype(jnp.bfloat16)

    @pl.loop(0, tiles + LAG + 1)
    def _(s):
        @pl.when(s < tiles)
        def _():
            wait_for(held.at[s], rx.at[s])
            send_yz(s)

        @pl.when(s + AHEAD < tiles)
        def _():
            send_x(s + AHEAD)

        @pl.when(s == 0)
        def _():
            wait_for(slab.at[:, pl.ds(0, 3), x], rs.at[1])
            for copy in slab_x():
                copy.start()

        @pl.when(jnp.logical_and(s >= LAG, s < tiles + LAG))
        def _():
            u = s - LAG
            wait_for(group(u, core), ry.at[u])
            forward(u).start()

        @pl.when(s == LAG)
        def _():
            prepare()

        @pl.when(s > LAG)
        def _():
            v = s - LAG - 1
            wait_for(group(v, 1 - core), rf.at[v])
            compute(v)

    @pl.when(is_source)
    def _():
        wait_for(tall.at[0, pl.ds(0, 7 * 64)], ss.at[0])
    for copy in slab_z():
        copy.wait_send()
    for copy in slab_x():
        copy.wait_send()

    @pl.loop(0, tiles)
    def _(t):
        wait_for(held.at[t].at[:, 0:96], sx.at[t])
        for dh in (1, 0):
            for l in range(2):
                yz(t, dh, l, False)
        forward(t).wait_send()


def per_device(slopes, covariance):
    frames, columns, rows = 1024, covariance.shape[1], covariance.shape[0]
    tiles = columns // WIDTH
    vmem = pl.BlockSpec(memory_space=pltpu.VMEM)
    hbm = pl.BlockSpec(memory_space=pl.ANY)
    dma = pltpu.SemaphoreType.DMA
    return pl.pallas_call(
        kernel,
        out_shape=pltpu.VMEM(covariance.shape, jnp.float32),
        in_specs=[hbm, hbm],
        out_specs=vmem,
        scratch_shapes=[
            pltpu.VMEM((tiles, 2, 128, WIDTH), jnp.float32),
            pltpu.VMEM((tiles, frames, WIDTH), jnp.float32),
            pltpu.VMEM((2, 4, 4, 32, rows), jnp.float32),
            pltpu.VMEM((rows, frames), jnp.bfloat16),
            pltpu.VMEM((rows, frames), jnp.bfloat16),
            dma((tiles,)), dma((tiles,)), dma((tiles,)), dma((tiles,)), dma((tiles,)), dma((tiles,)),
            dma((3,)), dma((3,)), dma, dma,
        ],
        compiler_params=pltpu.CompilerParams(
            collective_id=0, has_side_effects=True, vmem_limit_bytes=50 << 20
        ),
        cost_estimate=pl.CostEstimate(
            flops=6 * rows * frames * columns, bytes_accessed=24 << 20, transcendentals=0
        ),
        name="slab_update",
    )(slopes, covariance)


def solution(mesh):
    return jax.shard_map(
        per_device, mesh=mesh, in_specs=(P("col", "row"), P("row", "col")),
        out_specs=P("row", "col"), check_vma=False,
    )
```

```python
import functools

import jax
import jax.numpy as jnp
from jax import lax
from jax.experimental import pallas as pl
from jax.experimental.pallas import tpu as pltpu
from jax.sharding import PartitionSpec as P

MESH = pl.DeviceIdType.MESH
WIDTH = 512
AHEAD = 2
LAG_Z = 2
LAG = 5
SLAB_X, EVERY = 5, 1
FIRST = 21
ORDER = (2, 1, 3)


def kernel(
    slopes_hbm, cov, out, slopes, held, mid, tall, slab, slab_hi, slab_lo,
    sx, rx, sy, ry, sz, rz, sf, rf, ss, rs, cov_sem, own_sem,
):
    row, col = lax.axis_index("row"), lax.axis_index("col")
    x, y_lo, z = lax.rem(col, 4), lax.rem(lax.div(col, 4), 2), lax.div(col, 8)
    core, y_hi = lax.rem(row, 2), lax.div(row, 2)
    z_odd, z_hi = lax.rem(z, 2), lax.div(z, 2)
    y = y_hi * 2 + y_lo
    units, sources, depth, width = tall.shape
    deep = sources * depth
    block = units // 4 * width
    frames = 4 * deep

    def along_x(dx):
        return row, z * 8 + y_lo * 4 + lax.rem(x + dx, 4)

    def along_y(dy, k):
        to = lax.rem(y + dy, 4)
        return lax.div(to, 2) * 2 + k, z * 8 + lax.rem(to, 2) * 4 + x

    def along_z(dz, k):
        return y_hi * 2 + k, lax.rem(z + dz, 4) * 8 + y_lo * 4 + x

    own_copy = pltpu.make_async_copy(slopes_hbm, slopes, own_sem)
    own_copy.start()

    other = 1 - core
    partners = [along_x(d) for d in (1, 2, 3)] + [along_y(0, other)]
    for d in (1, 2, 3):
        for k in (core, other):
            partners += [along_y(d, k), along_z(d, k)]
    barrier = pltpu.get_barrier_semaphore()
    for partner in partners:
        pl.semaphore_signal(barrier, inc=1, device_id=partner, device_id_type=MESH)
    pl.semaphore_wait(barrier, len(partners))
    own_copy.wait()

    def remote(src, dst, send, recv, to):
        return pltpu.make_async_remote_copy(
            src_ref=src, dst_ref=dst, send_sem=send, recv_sem=recv,
            device_id=to, device_id_type=MESH,
        )

    def wait_for(ref, sem):
        pltpu.make_async_copy(ref, ref, sem).wait()

    cov_copy = pltpu.make_async_copy(cov, out, cov_sem)

    is_source = jnp.logical_and(y_hi == 0, core == 0)

    def slab_columns(r):
        return slopes.at[:, pl.ds(pl.multiple_of(r * 512, 512), 512)]

    @pl.when(is_source)
    def _():
        mine = slab.at[x, z_odd, z_hi, y_lo]
        pltpu.make_async_copy(slab_columns(row), mine, rs.at[0]).start()
        for dy, k in ((0, 1), (1, 0), (1, 1), (3, 0), (3, 1), (2, 0), (2, 1)):
            r, c = along_y(dy, k)
            remote(slab_columns(r), mine, ss.at[0], rs.at[0], (r, c)).start()

    def slab_z():
        mine = slab.at[x, z_odd, z_hi]
        return [remote(mine, mine, ss.at[1], rs.at[1], along_z(dz, core)) for dz in (2, 1, 3)]

    def slab_x(p):
        piece = slab.at[x, lax.div(p, 4), lax.rem(lax.div(p, 2), 2), lax.rem(p, 2)]
        return [remote(piece, piece, ss.at[2], rs.at[2], along_x(dx)) for dx in (2, 1, 3)]

    def place(u):
        n = lax.rem(u, 8)
        mine = lax.div(9 - n, 8)
        e = (n - 2) * (1 - mine)
        c = 2 * lax.div(u, 8) + mine * n + (1 - mine) * lax.div(e, 3)
        return c, (1 - mine) * (lax.rem(e, 3) + 1)

    def own(c, l, to):
        first = pl.multiple_of((l * 4 + to) * block + c * width, width)
        return slopes.at[:, pl.ds(first, width)]

    def send_x(c, dx):
        for l in range(2):
            src = own(c, l, lax.rem(x + 4 - dx, 4))
            remote(src, held.at[c, dx - 1, l], sx.at[c], rx.at[c, dx - 1], along_x(4 - dx)).start()

    def send_y(u, block_of):
        dst = mid.at[u, y]
        for dy in ORDER:
            remote(block_of(lax.rem(y_lo + dy, 2)), dst, sy.at[u], ry.at[u], along_y(dy, core)).start()
        pltpu.make_async_copy(block_of(y_lo), dst, ry.at[u]).start()

    def z_copy(t, j, start):
        src = mid.at[t, pl.ds(2 * j, 2)]
        dst = tall.at[t, pl.ds(pl.multiple_of(z_odd * 4 + z_hi * 2, 2), 2)]
        to = 2 * j + core
        is_self = jnp.logical_and(to == z, core == z_odd)
        if start:

            @pl.when(is_self)
            def _():
                pltpu.make_async_copy(src, dst, rz.at[t]).start()

        @pl.when(jnp.logical_not(is_self))
        def _():
            copy = remote(src, dst, sz.at[t], rz.at[t], (y_hi * 2 + z_odd, to * 8 + y_lo * 4 + x))
            if start:
                copy.start()
            else:
                copy.wait_send()

    def group(t, g):
        return tall.at[t, pl.ds(pl.multiple_of(g * 4, 4), 4)]

    def forward(t):
        mine = group(t, core)
        return remote(mine, mine, sf.at[t], rf.at[t], along_y(0, other))

    def prepare():
        cov_copy.wait()
        wait_for(slab.at[pl.ds(0, 3)], rs.at[2])
        for part in range(4):
            whole = slab[part].reshape(deep, slab.shape[5]).T
            hi = whole.astype(jnp.bfloat16)
            slab_hi[part] = hi
            slab_lo[part] = (whole - hi.astype(jnp.float32)).astype(jnp.bfloat16)

    def compute(u):
        wait_for(group(u, other), rf.at[u])
        c, d = place(u)
        part = lax.rem(x + d, 4)
        unit = tall[u].reshape(deep, width)
        hi = unit.astype(jnp.bfloat16)
        lo = (unit - hi.astype(jnp.float32)).astype(jnp.bfloat16)
        dot = functools.partial(jnp.dot, preferred_element_type=jnp.float32)
        product = dot(slab_hi[part], hi) + dot(slab_hi[part], lo) + dot(slab_lo[part], hi)
        columns = pl.ds(pl.multiple_of(c * width, width), width)
        out[:, columns] = out[:, columns] + product * (1.0 / frames**0.5)

    send_y(0, lambda l: own(0, l, x))
    for dx in (1, 2, 3):
        send_x(0, dx)
    wait_for(slab.at[x, z_odd, z_hi], rs.at[0])
    for copy in slab_z():
        copy.start()
    for c in range(1, AHEAD):
        for dx in (1, 2, 3):
            send_x(c, dx)
    cov_copy.start()

    even = 2 * FIRST - LAG - 1

    @pl.loop(0, units + LAG)
    def _(s):
        c, d = place(s)

        @pl.when(jnp.logical_and(d == 0, jnp.logical_and(s > 0, s < units)))
        def _():
            send_y(s, lambda l: own(c, l, x))

        @pl.when(jnp.logical_and(d > 0, s < units))
        def _():
            wait_for(held.at[c, d - 1], rx.at[c, d - 1])
            send_y(s, lambda l: held.at[c, d - 1, l])

        @pl.when(jnp.logical_and(d > 0, c + AHEAD < units // 4))
        def _():
            send_x(c + AHEAD, d)

        @pl.when(s == SLAB_X)
        def _():
            wait_for(tall.at[0, pl.ds(0, 6)], rs.at[1])

        p = lax.div(s - SLAB_X, EVERY)

        @pl.when(jnp.logical_and(jnp.logical_and(s >= SLAB_X, p < 8), lax.rem(s - SLAB_X, EVERY) == 0))
        def _():
            for copy in slab_x(p):
                copy.start()

        @pl.when(jnp.logical_and(s >= LAG_Z, s < units + LAG_Z))
        def _():
            t = s - LAG_Z
            wait_for(mid.at[t], ry.at[t])
            for j in range(2):
                z_copy(t, j, True)

        @pl.when(s == FIRST)
        def _():
            prepare()

        @pl.when(jnp.logical_and(s >= FIRST, s < even))
        def _():
            for i in range(2):
                compute((s - FIRST) * 2 + i)

        @pl.when(s >= even)
        def _():
            compute(s - LAG - 1)

        @pl.when(s >= LAG)
        def _():
            t = s - LAG
            wait_for(group(t, core), rz.at[t])
            forward(t).start()

    compute(units - 1)

    @pl.when(is_source)
    def _():
        wait_for(tall.at[0, pl.ds(0, 7)], ss.at[0])

    for copy in slab_z():
        copy.wait_send()
    wait_for(slab.at[pl.ds(0, 3)], ss.at[2])

    @pl.loop(0, units // 4)
    def _(c):
        wait_for(held.at[c], sx.at[c])

    @pl.loop(0, units)
    def _(t):
        wait_for(mid.at[t, pl.ds(0, 3)], sy.at[t])
        for j in range(2):
            z_copy(t, j, False)
        forward(t).wait_send()


def per_device(slopes, covariance):
    frames, columns, rows = 1024, covariance.shape[1], covariance.shape[0]
    units = 4 * (columns // WIDTH)
    depth = slopes.shape[0]
    hbm = pl.BlockSpec(memory_space=pl.ANY)
    dma = pltpu.SemaphoreType.DMA
    return pl.pallas_call(
        kernel,
        out_shape=pltpu.VMEM(covariance.shape, jnp.float32),
        in_specs=[hbm, hbm],
        out_specs=pl.BlockSpec(memory_space=pltpu.VMEM),
        scratch_shapes=[
            pltpu.VMEM(slopes.shape, jnp.float32),
            pltpu.VMEM((units // 4, 3, 2, depth, WIDTH), jnp.float32),
            pltpu.VMEM((units, 4, depth, WIDTH), jnp.float32),
            pltpu.VMEM((units, 8, depth, WIDTH), jnp.float32),
            pltpu.VMEM((4, 2, 2, 2, depth, rows), jnp.float32),
            pltpu.VMEM((4, rows, frames // 4), jnp.bfloat16),
            pltpu.VMEM((4, rows, frames // 4), jnp.bfloat16),
            dma((units // 4,)), dma((units // 4, 3)),
        ] + [dma((units,))] * 6 + [dma((3,)), dma((3,)), dma, dma],
        compiler_params=pltpu.CompilerParams(
            collective_id=0, has_side_effects=True, vmem_limit_bytes=50 << 20
        ),
        cost_estimate=pl.CostEstimate(
            flops=6 * rows * frames * columns, bytes_accessed=24 << 20, transcendentals=0
        ),
        name="slab_update",
    )(slopes, covariance)


def solution(mesh):
    return jax.shard_map(
        per_device, mesh=mesh, in_specs=(P("col", "row"), P("row", "col")),
        out_specs=P("row", "col"), check_vma=False,
    )
```

```python
import functools

import jax
import jax.numpy as jnp
from jax import lax
from jax.experimental import pallas as pl
from jax.experimental.pallas import tpu as pltpu
from jax.sharding import PartitionSpec as P

MESH = pl.DeviceIdType.MESH
WIDTH = 512
AHEAD = 2
LAG_Z = 2
LAG = 5
SLAB_X, EVERY = 5, 1
FIRST = 21
ORDER = (2, 1, 3)


def kernel(
    slopes_hbm, cov, out, slopes, held, mid, tall, slab, slab_hi, slab_lo,
    sx, rx, sy, ry, sz, rz, sf, rf, ss, rs, cov_sem, own_sem,
):
    row, col = lax.axis_index("row"), lax.axis_index("col")
    x, y_lo, z = lax.rem(col, 4), lax.rem(lax.div(col, 4), 2), lax.div(col, 8)
    core, y_hi = lax.rem(row, 2), lax.div(row, 2)
    z_odd, z_hi = lax.rem(z, 2), lax.div(z, 2)
    y = y_hi * 2 + y_lo
    units, sources, depth, width = tall.shape
    deep = sources * depth
    block = units // 4 * width
    frames = 4 * deep

    def along_x(dx):
        return row, z * 8 + y_lo * 4 + lax.rem(x + dx, 4)

    def along_y(dy, k):
        to = lax.rem(y + dy, 4)
        return lax.div(to, 2) * 2 + k, z * 8 + lax.rem(to, 2) * 4 + x

    def along_z(dz, k):
        return y_hi * 2 + k, lax.rem(z + dz, 4) * 8 + y_lo * 4 + x

    own_copy = pltpu.make_async_copy(slopes_hbm, slopes, own_sem)
    own_copy.start()

    other = 1 - core
    partners = [along_x(d) for d in (1, 2, 3)] + [along_y(0, other)]
    for d in (1, 2, 3):
        for k in (core, other):
            partners += [along_y(d, k), along_z(d, k)]
    barrier = pltpu.get_barrier_semaphore()
    for partner in partners:
        pl.semaphore_signal(barrier, inc=1, device_id=partner, device_id_type=MESH)
    pl.semaphore_wait(barrier, len(partners))
    own_copy.wait()

    def remote(src, dst, send, recv, to):
        return pltpu.make_async_remote_copy(
            src_ref=src, dst_ref=dst, send_sem=send, recv_sem=recv,
            device_id=to, device_id_type=MESH,
        )

    def wait_for(ref, sem):
        pltpu.make_async_copy(ref, ref, sem).wait()

    cov_copy = pltpu.make_async_copy(cov, out, cov_sem)

    is_source = jnp.logical_and(y_hi == 0, core == 0)

    def slab_columns(r):
        return slopes.at[:, pl.ds(pl.multiple_of(r * 512, 512), 512)]

    @pl.when(is_source)
    def _():
        mine = slab.at[x, z_odd, z_hi, y_lo]
        pltpu.make_async_copy(slab_columns(row), mine, rs.at[0]).start()
        for dy, k in ((0, 1), (1, 0), (1, 1), (3, 0), (3, 1), (2, 0), (2, 1)):
            r, c = along_y(dy, k)
            remote(slab_columns(r), mine, ss.at[0], rs.at[0], (r, c)).start()

    def slab_z():
        mine = slab.at[x, z_odd, z_hi]
        return [remote(mine, mine, ss.at[1], rs.at[1], along_z(dz, core)) for dz in (2, 1, 3)]

    def slab_x(p):
        piece = slab.at[x, lax.div(p, 4), lax.rem(lax.div(p, 2), 2), lax.rem(p, 2)]
        return [remote(piece, piece, ss.at[2], rs.at[2], along_x(dx)) for dx in (2, 1, 3)]

    def place(u):
        n = lax.rem(u, 8)
        mine = lax.div(9 - n, 8)
        e = (n - 2) * (1 - mine)
        c = 2 * lax.div(u, 8) + mine * n + (1 - mine) * lax.div(e, 3)
        return c, (1 - mine) * (lax.rem(e, 3) + 1)

    def own(c, l, to):
        first = pl.multiple_of((l * 4 + to) * block + c * width, width)
        return slopes.at[:, pl.ds(first, width)]

    def send_x(c, dx):
        for l in range(2):
            src = own(c, l, lax.rem(x + 4 - dx, 4))
            remote(src, held.at[c, dx - 1, l], sx.at[c], rx.at[c, dx - 1], along_x(4 - dx)).start()

    def send_y(u, block_of):
        dst = mid.at[u, y]
        for dy in ORDER:
            remote(block_of(lax.rem(y_lo + dy, 2)), dst, sy.at[u], ry.at[u], along_y(dy, core)).start()
        pltpu.make_async_copy(block_of(y_lo), dst, ry.at[u]).start()

    def z_copy(t, j, start):
        src = mid.at[t, pl.ds(2 * j, 2)]
        dst = tall.at[t, pl.ds(pl.multiple_of(z_odd * 4 + z_hi * 2, 2), 2)]
        to = 2 * j + core
        is_self = jnp.logical_and(to == z, core == z_odd)
        if start:

            @pl.when(is_self)
            def _():
                pltpu.make_async_copy(src, dst, rz.at[t]).start()

        @pl.when(jnp.logical_not(is_self))
        def _():
            copy = remote(src, dst, sz.at[t], rz.at[t], (y_hi * 2 + z_odd, to * 8 + y_lo * 4 + x))
            if start:
                copy.start()
            else:
                copy.wait_send()

    def group(t, g):
        return tall.at[t, pl.ds(pl.multiple_of(g * 4, 4), 4)]

    def forward(t):
        mine = group(t, core)
        return remote(mine, mine, sf.at[t], rf.at[t], along_y(0, other))

    def prepare():
        cov_copy.wait()
        wait_for(slab.at[pl.ds(0, 3)], rs.at[2])
        for part in range(4):
            whole = slab[part].reshape(deep, slab.shape[5]).T
            hi = whole.astype(jnp.bfloat16)
            slab_hi[part] = hi
            slab_lo[part] = (whole - hi.astype(jnp.float32)).astype(jnp.bfloat16)

    def compute(u):
        wait_for(group(u, other), rf.at[u])
        c, d = place(u)
        part = lax.rem(x + d, 4)
        unit = tall[u].reshape(deep, width)
        hi = unit.astype(jnp.bfloat16)
        lo = (unit - hi.astype(jnp.float32)).astype(jnp.bfloat16)
        dot = functools.partial(jnp.dot, preferred_element_type=jnp.float32)
        product = dot(slab_hi[part], hi) + dot(slab_hi[part], lo) + dot(slab_lo[part], hi)
        columns = pl.ds(pl.multiple_of(c * width, width), width)
        out[:, columns] = out[:, columns] + product * (1.0 / frames**0.5)

    send_y(0, lambda l: own(0, l, x))
    for dx in (1, 2, 3):
        send_x(0, dx)
    wait_for(slab.at[x, z_odd, z_hi], rs.at[0])
    for copy in slab_z():
        copy.start()
    for c in range(1, AHEAD):
        for dx in (1, 2, 3):
            send_x(c, dx)
    cov_copy.start()

    def sent(t):
        wait_for(mid.at[t, pl.ds(0, 3)], sy.at[t])
        for j in range(2):
            z_copy(t, j, False)
        forward(t).wait_send()

    even = 2 * FIRST - LAG - 1

    @pl.loop(0, units + LAG)
    def _(s):
        c, d = place(s)

        @pl.when(jnp.logical_and(d == 0, jnp.logical_and(s > 0, s < units)))
        def _():
            send_y(s, lambda l: own(c, l, x))

        @pl.when(jnp.logical_and(d > 0, s < units))
        def _():
            wait_for(held.at[c, d - 1], rx.at[c, d - 1])
            send_y(s, lambda l: held.at[c, d - 1, l])

        @pl.when(jnp.logical_and(d > 0, c + AHEAD < units // 4))
        def _():
            send_x(c + AHEAD, d)

        @pl.when(s == SLAB_X)
        def _():
            wait_for(tall.at[0, pl.ds(0, 6)], rs.at[1])

        p = lax.div(s - SLAB_X, EVERY)

        @pl.when(jnp.logical_and(jnp.logical_and(s >= SLAB_X, p < 8), lax.rem(s - SLAB_X, EVERY) == 0))
        def _():
            for copy in slab_x(p):
                copy.start()

        @pl.when(jnp.logical_and(s >= LAG_Z, s < units + LAG_Z))
        def _():
            t = s - LAG_Z
            wait_for(mid.at[t], ry.at[t])
            for j in range(2):
                z_copy(t, j, True)

        @pl.when(s == FIRST)
        def _():
            prepare()

        @pl.when(jnp.logical_and(s >= FIRST, s < even))
        def _():
            for i in range(2):
                compute((s - FIRST) * 2 + i)

        @pl.when(s >= even)
        def _():
            compute(s - LAG - 1)

        @pl.when(s >= LAG)
        def _():
            t = s - LAG
            wait_for(group(t, core), rz.at[t])
            forward(t).start()

        @pl.when(s > LAG)
        def _():
            sent(s - LAG - 1)

    @pl.when(is_source)
    def _():
        wait_for(tall.at[0, pl.ds(0, 7)], ss.at[0])

    for copy in slab_z():
        copy.wait_send()
    wait_for(slab.at[pl.ds(0, 3)], ss.at[2])

    @pl.loop(0, units // 4)
    def _(c):
        wait_for(held.at[c], sx.at[c])

    compute(units - 1)
    sent(units - 1)


def per_device(slopes, covariance):
    frames, columns, rows = 1024, covariance.shape[1], covariance.shape[0]
    units = 4 * (columns // WIDTH)
    depth = slopes.shape[0]
    hbm = pl.BlockSpec(memory_space=pl.ANY)
    dma = pltpu.SemaphoreType.DMA
    return pl.pallas_call(
        kernel,
        out_shape=pltpu.VMEM(covariance.shape, jnp.float32),
        in_specs=[hbm, hbm],
        out_specs=pl.BlockSpec(memory_space=pltpu.VMEM),
        scratch_shapes=[
            pltpu.VMEM(slopes.shape, jnp.float32),
            pltpu.VMEM((units // 4, 3, 2, depth, WIDTH), jnp.float32),
            pltpu.VMEM((units, 4, depth, WIDTH), jnp.float32),
            pltpu.VMEM((units, 8, depth, WIDTH), jnp.float32),
            pltpu.VMEM((4, 2, 2, 2, depth, rows), jnp.float32),
            pltpu.VMEM((4, rows, frames // 4), jnp.bfloat16),
            pltpu.VMEM((4, rows, frames // 4), jnp.bfloat16),
            dma((units // 4,)), dma((units // 4, 3)),
        ] + [dma((units,))] * 6 + [dma((3,)), dma((3,)), dma, dma],
        compiler_params=pltpu.CompilerParams(
            collective_id=0, has_side_effects=True, vmem_limit_bytes=50 << 20
        ),
        cost_estimate=pl.CostEstimate(
            flops=6 * rows * frames * columns, bytes_accessed=24 << 20, transcendentals=0
        ),
        name="slab_update",
    )(slopes, covariance)


def solution(mesh):
    return jax.shard_map(
        per_device, mesh=mesh, in_specs=(P("col", "row"), P("row", "col")),
        out_specs=P("row", "col"), check_vma=False,
    )
```
